128 devices in a mesh: col: 8 (over y, core), row: 16 (over z, x).
Axes of the slice: x: 4, y: 4, z: 4, core: 2. Of those that a mesh axis runs over, the one named last changes fastest.
Arguments:
- snapshots: float32 [65536, 2048], P('row', 'col'), may hold values from -80 to 80
- orientation: int32 [2, 8], replicated, may hold values from 0 to 1
Outputs:
- rotated: float32 [65536, 2048], P('row', 'col')
- basis: float32 [2048, 2048], P('row', 'col')
The draws below stay inside these ranges and needn't reach their ends.
All inputs are finite; a program needn't handle non-finite values.
Results may differ from the reference program's by a relative error of at most 0.00065.
Values sent between devices are 32-bit elements; how exact they have to be, the bound alone decides.
A program may use at most 64 MiB of HBM per device.

```python
import jax
import jax.numpy as jnp
from jax import lax

BW = 128
STEPS = 24
ROUNDS = 2
GROUPS = 8
N = 2048
ROWS = 65536


def draw_snapshots(key, part):
    key = jax.random.fold_in(key, 11)
    noise_key, row_key, column_key = jax.random.split(key, 3)
    row_fraction = jnp.arange(ROWS, dtype=jnp.float32) / ROWS
    row_scale = (3.0 ** row_fraction)[:, None] * 10.0 ** (jax.random.uniform(row_key, (ROWS, 1), dtype=jnp.float32) - 0.75)
    column_scale = 0.3 * 10.0 ** jax.random.uniform(column_key, (1, N), dtype=jnp.float32)
    base_noise = jnp.clip(jax.random.normal(noise_key, (ROWS, N), dtype=jnp.float32), -5.0, 5.0)
    return (base_noise * row_scale * column_scale).astype(jnp.float32)


def place_ends(values, stream_key, least, high):
    shape = values.shape
    place = [jax.random.randint(jax.random.fold_in(stream_key, axis), (), 0, shape[axis]) for axis in range(len(shape))]
    values = values.at[tuple(place)].set(least)
    longest = shape.index(max(shape))
    place[longest] = (place[longest] + 1) % shape[longest]
    return values.at[tuple(place)].set(high)


def setup_inputs(seed: int = 0) -> dict:
    splits = jax.random.split(jax.random.key(seed), 3)
    snapshots = draw_snapshots(jax.random.fold_in(splits[2], 71), 0)
    orientation = place_ends(jax.random.randint(splits[1], (ROUNDS, GROUPS), 0, 2), jax.random.fold_in(splits[1], 1), 0, 1).astype(jnp.int32)
    return dict(snapshots=snapshots, orientation=orientation)


def turn_columns(matrix, cosine, sine_value):
    half_width = cosine.shape[0]
    left_half = matrix[:, :half_width]
    right_half = matrix[:, half_width:]
    first_part = left_half * cosine[None, :] - right_half * sine_value[None, :]
    second_part = left_half * sine_value[None, :] + right_half * cosine[None, :]
    return jnp.concatenate([first_part[:, :1], second_part[:, :1], first_part[:, 1:half_width - 1], second_part[:, 1:], first_part[:, half_width - 1:]], 1)

def jacobi_steps(gram_matrix, step_count):
    half_width = gram_matrix.shape[0] // 2

    def rotation_step(step_index, loop_state):
        current, rotation = loop_state
        first_diag = jnp.diagonal(current[:half_width, :half_width])
        second_diag = jnp.diagonal(current[half_width:, half_width:])
        coupling = jnp.diagonal(current[:half_width, half_width:])
        spread = second_diag - first_diag
        orient_sign = jnp.where(spread >= 0.0, 1.0, -1.0).astype(jnp.float32)
        tangent = orient_sign * 2.0 * coupling / (jnp.abs(spread) + jnp.sqrt(spread * spread + 4.0 * coupling * coupling))
        cosine = 1.0 / jnp.sqrt(1.0 + tangent * tangent)
        sine_value = tangent * cosine
        right_side = turn_columns(current, cosine, sine_value)
        current = turn_columns(right_side.T, cosine, sine_value).T
        rotation = turn_columns(rotation, cosine, sine_value)
        return (current, rotation)
    start = jnp.eye(2 * half_width, dtype=jnp.float32)
    return lax.fori_loop(0, step_count, rotation_step, (gram_matrix, start))

def rotate_pair(pair_blocks):
    upper_block, lower_block, upper_basis, lower_basis = pair_blocks
    joined = jnp.concatenate([upper_block, lower_block], 1)
    gram_matrix = lax.dot_general(joined, joined, (((0,), (0,)), ((), ())), precision=lax.Precision.HIGHEST, preferred_element_type=jnp.float32)
    final_gram, rotation = jacobi_steps(gram_matrix, STEPS)
    turned = jnp.dot(joined, rotation, precision=lax.Precision.HIGHEST, preferred_element_type=jnp.float32)
    basis_joined = jnp.concatenate([upper_basis, lower_basis], 1)
    basis_turned = jnp.dot(basis_joined, rotation, precision=lax.Precision.HIGHEST, preferred_element_type=jnp.float32)
    return (turned[:, :BW], turned[:, BW:], basis_turned[:, :BW], basis_turned[:, BW:])

def move_slots(upper_all, lower_all):
    new_upper = jnp.concatenate([upper_all[:1], lower_all[:1], upper_all[1:-1]], 0)
    new_lower = jnp.concatenate([lower_all[1:], upper_all[-1:]], 0)
    return (new_upper, new_lower)

def reference(snapshots, orientation):
    slots = snapshots.reshape(ROWS, GROUPS, 2, BW).transpose(1, 2, 0, 3)
    upper_all = slots[:, 0]
    lower_all = slots[:, 1]
    eye_slots = jnp.eye(N, dtype=jnp.float32).reshape(N, GROUPS, 2, BW).transpose(1, 2, 0, 3)
    basis_upper = eye_slots[:, 0]
    basis_lower = eye_slots[:, 1]
    for round_index in range(ROUNDS):
        flipped = (orientation[round_index] == 1)[:, None, None]
        upper_all, lower_all = (jnp.where(flipped, lower_all, upper_all), jnp.where(flipped, upper_all, lower_all))
        basis_upper, basis_lower = (jnp.where(flipped, basis_lower, basis_upper), jnp.where(flipped, basis_upper, basis_lower))
        upper_all, lower_all, basis_upper, basis_lower = lax.map(rotate_pair, (upper_all, lower_all, basis_upper, basis_lower))
        if round_index + 1 < ROUNDS:
            upper_all, lower_all = move_slots(upper_all, lower_all)
            basis_upper, basis_lower = move_slots(basis_upper, basis_lower)
    rotated = jnp.stack([upper_all, lower_all], 1).transpose(2, 0, 1, 3).reshape(ROWS, N)
    basis = jnp.stack([basis_upper, basis_lower], 1).transpose(2, 0, 1, 3).reshape(N, N)
    return (rotated, basis)
```

```python
import functools

import jax
import jax.numpy as jnp
from jax import lax
from jax.experimental import pallas as pl
from jax.experimental.pallas import tpu as pltpu
from jax.sharding import PartitionSpec as P

STEPS = 24
H = 128
F32 = jnp.float32
BF16 = jnp.bfloat16
MESH = pl.DeviceIdType.MESH
RAW = 1280
CHUNK = 256


def sublane_total(x):
    x = x + pltpu.roll(x, 4, 0)
    x = x + pltpu.roll(x, 2, 0)
    return x + pltpu.roll(x, 1, 0)


def diagonal(block):
    lane = lax.broadcasted_iota(jnp.int32, (8, H), 1)
    sub = lax.broadcasted_iota(jnp.int32, (8, H), 0)
    acc = jnp.zeros((8, H), F32)
    for i in range(H // 8):
        acc = jnp.where((lane >> 3) == i, block[8 * i : 8 * i + 8, :], acc)
    return sublane_total(jnp.where((lane & 7) == sub, acc, 0.0))


def angles(a, b, d):
    e = b - a
    sign = jnp.where(e >= 0.0, 2.0, -2.0)
    t = sign * d / (jnp.abs(e) + jnp.sqrt(e * e + 4.0 * d * d))
    c = 1.0 / jnp.sqrt(1.0 + t * t)
    return c, t * c


def jacobi(gram, turn):
    lane = lax.broadcasted_iota(jnp.int32, (H, H), 1)
    row = lax.broadcasted_iota(jnp.int32, (H, H), 0)
    eye = (lane == row).astype(F32)
    turn[0] = eye
    turn[1] = jnp.zeros((H, H), F32)
    turn[2] = jnp.zeros((H, H), F32)
    turn[3] = eye

    def rows(top, bottom, c, s):
        f = top * c - bottom * s
        g = top * s + bottom * c
        x = jnp.where(row == 0, g, f)
        u = jnp.where(row == 0, f, pltpu.roll(x, 1, 0))
        v = jnp.where(row == H - 1, f, pltpu.roll(g, H - 1, 0))
        return u, v

    def columns(left, right, c, s):
        f = left * c - right * s
        g = left * s + right * c
        x = jnp.where(lane == 0, g, f)
        u = jnp.where(lane == 0, f, pltpu.roll(x, 1, 1))
        v = jnp.where(lane == H - 1, f, pltpu.roll(g, H - 1, 1))
        return u, v

    def step(_, carry):
        c, s = angles(diagonal(gram[0]), diagonal(gram[3]), diagonal(gram[1]))
        c = jnp.broadcast_to(c[:1], (H, H))
        s = jnp.broadcast_to(s[:1], (H, H))
        ct = jnp.transpose(c)
        st = jnp.transpose(s)
        ut, vt = columns(gram[0], gram[1], c, s)
        ub, vb = columns(gram[2], gram[3], c, s)
        gram[0], gram[2] = rows(ut, ub, ct, st)
        gram[1], gram[3] = rows(vt, vb, ct, st)
        turn[0], turn[2] = rows(turn[0], turn[2], ct, st)
        turn[1], turn[3] = rows(turn[1], turn[3], ct, st)
        return carry

    lax.fori_loop(0, STEPS, step, 0)


def load_gram(gram, a, c, d, flipped):
    ct = jnp.transpose(c)
    gram[0] = jnp.where(flipped, d, a)
    gram[1] = jnp.where(flipped, ct, c)
    gram[2] = jnp.where(flipped, c, ct)
    gram[3] = jnp.where(flipped, a, d)


def rotation(turn, flipped):
    t0, t1, t2, t3 = turn[0], turn[1], turn[2], turn[3]
    up = jnp.concatenate([jnp.where(flipped, t1, t0), jnp.where(flipped, t0, t1)], 1)
    lo = jnp.concatenate([jnp.where(flipped, t3, t2), jnp.where(flipped, t2, t3)], 1)
    return jnp.transpose(up), jnp.transpose(lo)


def split(x):
    hi = x.astype(BF16)
    lo = (x - hi.astype(F32)).astype(BF16)
    return hi, lo


def dot(x, y):
    return lax.dot_general(x, y, (((1,), (0,)), ((), ())), preferred_element_type=F32)


def dot_t(x, y):
    return lax.dot_general(x, y, (((0,), (0,)), ((), ())), preferred_element_type=F32)


def product(x, w_hi, w_lo):
    hi, lo = split(x)
    return dot(hi, w_hi) + (dot(hi, w_lo) + dot(lo, w_hi))


def first_kernel(
    n_col, n_row,
    x_ref, ori_ref,
    u_out, l_out, pack_l_out, pack_r_out, c_out,
    b, raw_l, raw_r, u2, l2, send_r, send_x, acc, part, rs_buf, total, gram, turn,
    pack_send, pack_l, pack_r, w_hi, w_lo, acc2, part2, rs2_buf, total2,
    load_sem, rs_send, rs_recv, ag_send, ag_recv, rs2_send, rs2_recv, ag2_send, ag2_recv,
    raw_send, raw_recv, pack_ssem, pack_rsem, r_send, r_recv, x_send, x_recv, out_sem,
):
    rows = b.shape[0]
    col = lax.axis_index("col")
    row = lax.axis_index("row")
    first = col == 0
    last = col == n_col - 1
    right = lax.rem(col + 1, n_col)
    left = lax.rem(col + n_col - 1, n_col)

    barrier = pltpu.get_barrier_semaphore()
    for o in range(1, n_row):
        pl.semaphore_signal(
            barrier, inc=1, device_id={"row": lax.rem(row + o, n_row)}, device_id_type=MESH
        )
    for side in (left, right):
        pl.semaphore_signal(barrier, inc=1, device_id={"col": side}, device_id_type=MESH)

    n_load = load_sem.shape[0]
    step = rows // n_load

    def load(i):
        part_rows = pl.ds(pl.multiple_of(i * step, 8), step)
        return pltpu.make_async_copy(x_ref.at[part_rows], b.at[part_rows], load_sem.at[i])

    for i in range(n_load):
        load(i).start()

    def right_start(src, dst, ssem, rsem):
        @pl.when(jnp.logical_not(last))
        def _():
            pltpu.make_async_remote_copy(
                src, dst[0], ssem, rsem.at[0], device_id={"col": right}, device_id_type=MESH
            ).start()

        @pl.when(last)
        def _():
            pltpu.make_async_copy(src, dst[1], rsem.at[1]).start()

    def left_start(src, dst, ssem, rsem):
        @pl.when(jnp.logical_not(first))
        def _():
            pltpu.make_async_remote_copy(
                src, dst[1], ssem, rsem.at[1], device_id={"col": left}, device_id_type=MESH
            ).start()

        @pl.when(first)
        def _():
            pltpu.make_async_copy(src, dst[0], rsem.at[0]).start()

    def arrived(dst, sem):
        pltpu.make_async_copy(dst, dst, sem).wait()

    def right_sent(src, ssem):
        @pl.when(jnp.logical_not(last))
        def _():
            pltpu.make_async_copy(src, src, ssem).wait()

    def left_sent(src, ssem):
        @pl.when(jnp.logical_not(first))
        def _():
            pltpu.make_async_copy(src, src, ssem).wait()

    acc[...] = jnp.zeros_like(acc)

    def gram_part(i):
        load(i).wait()
        hi, lo = split(b[pl.ds(pl.multiple_of(i * step, 8), step), :])
        acc[...] += dot_t(hi, jnp.concatenate([hi, lo], 1))

    n_first = -(-RAW // step)
    lax.fori_loop(0, n_first, lambda i, c: (gram_part(i), c)[1], 0)
    pl.semaphore_wait(barrier, n_row + 1)
    raw_src = b.at[pl.ds(0, RAW)]
    right_start(raw_src, (raw_l, raw_r), raw_send.at[0], raw_recv)
    left_start(raw_src, (raw_l, raw_r), raw_send.at[1], raw_recv)
    lax.fori_loop(n_first, n_load, lambda i, c: (gram_part(i), c)[1], 0)
    cross = acc[:H, 3 * H :] + jnp.transpose(acc[H:, 2 * H : 3 * H])
    part[:H] = acc[:H, :H] + (acc[:H, 2 * H : 3 * H] + jnp.transpose(acc[:H, 2 * H : 3 * H]))
    part[H : 2 * H] = acc[:H, H : 2 * H] + cross
    part[2 * H :] = acc[H:, H : 2 * H] + (acc[H:, 3 * H :] + jnp.transpose(acc[H:, 3 * H :]))

    def all_reduce(local, buf, whole, s_send, s_recv, g_send, g_recv):
        size = buf.shape[1]
        mine = pl.ds(pl.multiple_of(row * size, 8), size)

        def scatter(o):
            peer = lax.rem(row + o, n_row)
            return pltpu.make_async_remote_copy(
                local.at[pl.ds(pl.multiple_of(peer * size, 8), size)], buf.at[o],
                s_send.at[o], s_recv.at[o], device_id={"row": peer}, device_id_type=MESH,
            )

        def gather(o):
            peer = lax.rem(row + o, n_row)
            return pltpu.make_async_remote_copy(
                whole.at[mine], whole.at[mine],
                g_send.at[o], g_recv.at[o], device_id={"row": peer}, device_id_type=MESH,
            )

        for o in range(1, n_row):
            scatter(o).start()
        value = local[mine, :]
        for o in range(1, n_row):
            scatter(o).wait_recv()
            value = value + buf[o]
        whole[mine, :] = value
        for o in range(1, n_row):
            gather(o).start()
        for o in range(1, n_row):
            gather(o).wait_recv()
        for o in range(1, n_row):
            scatter(o).wait_send()
            gather(o).wait_send()

    all_reduce(part, rs_buf, total, rs_send, rs_recv, ag_send, ag_recv)

    flipped = ori_ref[0, col] == 1
    load_gram(gram, total[:H], total[H : 2 * H], total[2 * H :], flipped)
    jacobi(gram, turn)
    up, lo = rotation(turn, flipped)
    w_r = jnp.where(first, lo, up)
    w_x = jnp.where(first, up, lo)
    pack_send[0, : 2 * H] = w_r
    pack_send[0, 2 * H :] = jnp.where(first, gram[3], gram[0])
    pack_send[1, : 2 * H] = w_x
    pack_send[1, 2 * H :] = jnp.where(first, gram[0], gram[3])
    right_start(pack_send.at[0], (pack_l, pack_r), pack_ssem.at[0], pack_rsem)
    left_start(pack_send.at[1], (pack_l, pack_r), pack_ssem.at[1], pack_rsem)
    hi, lo = split(jnp.concatenate([w_r, w_x], 1))
    w_hi[...] = hi
    w_lo[...] = lo

    n_turn = (rows - RAW) // CHUNK

    def late(i):
        return pl.ds(pl.multiple_of(RAW + i * CHUNK, 8), CHUNK)

    def sent(i):
        return pl.ds(pl.multiple_of(i * CHUNK, 8), CHUNK)

    def turn_part(i, carry):
        turned = product(b[late(i), :], w_hi[...], w_lo[...])
        send_r[sent(i), :] = turned[:, :H]
        send_x[sent(i), :] = turned[:, H:]
        dst = (u2.at[late(i)], l2.at[late(i)])
        right_start(send_r.at[sent(i)], dst, r_send.at[i], r_recv.at[i])
        left_start(send_x.at[sent(i)], dst, x_send.at[i], r_recv.at[i])
        return carry

    lax.fori_loop(0, n_turn, turn_part, 0)

    acc2[...] = jnp.zeros_like(acc2)

    def cross_part(at):
        u_hi, u_lo = split(u2[at, :])
        l_hi, l_lo = split(l2[at, :])
        acc2[...] += dot_t(
            jnp.concatenate([u_hi, u_lo], 1), jnp.concatenate([l_hi, l_lo], 1)
        )
        slot = at.start // CHUNK
        pltpu.make_async_copy(u2.at[at], u_out.at[at], out_sem.at[0, slot]).start()
        pltpu.make_async_copy(l2.at[at], l_out.at[at], out_sem.at[1, slot]).start()

    arrived(raw_l, raw_recv.at[0])
    arrived(raw_r, raw_recv.at[1])
    arrived(pack_l, pack_rsem.at[0])
    arrived(pack_r, pack_rsem.at[1])
    out_l = pltpu.make_async_copy(pack_l, pack_l_out, out_sem.at[0, rows // CHUNK])
    out_r = pltpu.make_async_copy(pack_r, pack_r_out, out_sem.at[1, rows // CHUNK])
    out_l.start()
    out_r.start()
    wl_hi, wl_lo = split(pack_l[: 2 * H])
    wr_hi, wr_lo = split(pack_r[: 2 * H])
    w_hi[...] = jnp.concatenate([wl_hi, wr_hi], 1)
    w_lo[...] = jnp.concatenate([wl_lo, wr_lo], 1)

    def raw_part(i, carry):
        at = pl.ds(pl.multiple_of(i * CHUNK, 8), CHUNK)
        u2[at, :] = product(raw_l[at, :], w_hi[:, :H], w_lo[:, :H])
        l2[at, :] = product(raw_r[at, :], w_hi[:, H:], w_lo[:, H:])
        cross_part(at)
        return carry

    lax.fori_loop(0, RAW // CHUNK, raw_part, 0)

    def late_part(i, carry):
        arrived(u2.at[late(i)], r_recv.at[i, 0])
        arrived(l2.at[late(i)], r_recv.at[i, 1])
        cross_part(late(i))
        return carry

    lax.fori_loop(0, n_turn, late_part, 0)
    part2[...] = (acc2[:H, :H] + acc2[H:, H:]) + (acc2[:H, H:] + acc2[H:, :H])
    all_reduce(part2, rs2_buf, total2, rs2_send, rs2_recv, ag2_send, ag2_recv)
    out_c = pltpu.make_async_copy(total2, c_out, load_sem.at[0])
    out_c.start()

    right_sent(raw_src, raw_send.at[0])
    left_sent(raw_src, raw_send.at[1])
    right_sent(pack_send.at[0], pack_ssem.at[0])
    left_sent(pack_send.at[1], pack_ssem.at[1])

    def drain(i, carry):
        right_sent(send_r.at[sent(i)], r_send.at[i])
        left_sent(send_x.at[sent(i)], x_send.at[i])
        return carry

    lax.fori_loop(0, n_turn, drain, 0)

    def written(i, carry):
        at = pl.ds(pl.multiple_of(i * CHUNK, 8), CHUNK)
        pltpu.make_async_copy(u2.at[at], u_out.at[at], out_sem.at[0, i]).wait()
        pltpu.make_async_copy(l2.at[at], l_out.at[at], out_sem.at[1, i]).wait()
        return carry

    lax.fori_loop(0, rows // CHUNK, written, 0)
    out_l.wait()
    out_r.wait()
    out_c.wait()


def first_round(n_col, n_row, snapshots, orientation):
    rows = snapshots.shape[0]
    late = rows - RAW
    n_turn = late // CHUNK
    sem = pltpu.SemaphoreType.DMA
    any_spec = pl.BlockSpec(memory_space=pl.ANY)
    return pl.pallas_call(
        functools.partial(first_kernel, n_col, n_row),
        out_shape=[
            jax.ShapeDtypeStruct((rows, H), F32),
            jax.ShapeDtypeStruct((rows, H), F32),
            jax.ShapeDtypeStruct((3 * H, H), F32),
            jax.ShapeDtypeStruct((3 * H, H), F32),
            jax.ShapeDtypeStruct((H, H), F32),
        ],
        in_specs=[any_spec, pl.BlockSpec(memory_space=pltpu.SMEM)],
        out_specs=[any_spec] * 5,
        scratch_shapes=[
            pltpu.VMEM((rows, 2 * H), F32),
            pltpu.VMEM((RAW, 2 * H), F32),
            pltpu.VMEM((RAW, 2 * H), F32),
            pltpu.VMEM((rows, H), F32),
            pltpu.VMEM((rows, H), F32),
            pltpu.VMEM((late, H), F32),
            pltpu.VMEM((late, H), F32),
            pltpu.VMEM((2 * H, 4 * H), F32),
            pltpu.VMEM((3 * H, H), F32),
            pltpu.VMEM((n_row, 3 * H // n_row, H), F32),
            pltpu.VMEM((3 * H, H), F32),
            pltpu.VMEM((4, H, H), F32),
            pltpu.VMEM((4, H, H), F32),
            pltpu.VMEM((2, 3 * H, H), F32),
            pltpu.VMEM((3 * H, H), F32),
            pltpu.VMEM((3 * H, H), F32),
            pltpu.VMEM((2 * H, 2 * H), BF16),
            pltpu.VMEM((2 * H, 2 * H), BF16),
            pltpu.VMEM((2 * H, 2 * H), F32),
            pltpu.VMEM((H, H), F32),
            pltpu.VMEM((n_row, H // n_row, H), F32),
            pltpu.VMEM((H, H), F32),
            sem((8,)),
            sem((n_row,)), sem((n_row,)), sem((n_row,)), sem((n_row,)),
            sem((n_row,)), sem((n_row,)), sem((n_row,)), sem((n_row,)),
            sem((2,)), sem((2,)), sem((2,)), sem((2,)),
            sem((n_turn,)), sem((n_turn, 2)), sem((n_turn,)), sem((1,)),
            sem((2, rows // CHUNK + 1)),
        ],
        compiler_params=pltpu.CompilerParams(
            collective_id=0, has_side_effects=True, vmem_limit_bytes=48 * 2**20
        ),
    )(snapshots, orientation)


def last_kernel(
    n_col,
    u_ref, l_ref, pack_l, pack_r, c_ref, ori_ref,
    out_ref, basis_ref,
    u, l, out, basis, gram, turn, w_hi, w_lo, load_sem, out_sem,
):
    rows = u.shape[0]
    col = lax.axis_index("col")
    row = lax.axis_index("row")
    load_u = pltpu.make_async_copy(u_ref, u, load_sem.at[0])
    load_l = pltpu.make_async_copy(l_ref, l, load_sem.at[1])
    load_u.start()
    load_l.start()
    flipped = ori_ref[1, col] == 1
    load_gram(gram, pack_l[2 * H :], c_ref[...], pack_r[2 * H :], flipped)
    jacobi(gram, turn)
    up, lo = rotation(turn, flipped)
    hi, lo = split(jnp.concatenate([up, lo], 1))
    w_hi[...] = hi
    w_lo[...] = lo

    def finish(at):
        return pltpu.make_async_copy(out.at[at], out_ref.at[at], out_sem.at[at.start // CHUNK])

    load_u.wait()
    load_l.wait()

    def turn_part(i, carry):
        at = pl.ds(pl.multiple_of(i * CHUNK, 8), CHUNK)
        joined = jnp.concatenate([u[at, :], l[at, :]], 1)
        out[at, :] = product(joined, w_hi[...], w_lo[...])
        finish(at).start()
        return carry

    lax.fori_loop(0, rows // CHUNK, turn_part, 0)

    group = row // 2
    lower_half = row % 2 == 1
    from_left = jnp.maximum(col - 1, 0)
    from_right = jnp.minimum(col + 1, n_col - 1)
    basis_l = jnp.where(lower_half, pack_l[H : 2 * H], pack_l[:H])
    basis_r = jnp.where(lower_half, pack_r[H : 2 * H], pack_r[:H])
    basis_l = jnp.where(group == from_left, basis_l, 0.0)
    basis_r = jnp.where(group == from_right, basis_r, 0.0)
    basis[...] = product(jnp.concatenate([basis_l, basis_r], 1), w_hi[...], w_lo[...])
    out_basis = pltpu.make_async_copy(basis, basis_ref, load_sem.at[0])
    out_basis.start()

    def written(i, carry):
        finish(pl.ds(pl.multiple_of(i * CHUNK, 8), CHUNK)).wait()
        return carry

    lax.fori_loop(0, rows // CHUNK, written, 0)
    out_basis.wait()


def last_round(n_col, n_row, u2, l2, pack_l, pack_r, cross, orientation):
    rows = u2.shape[0]
    basis_rows = 2 * H * n_col // n_row
    sem = pltpu.SemaphoreType.DMA
    any_spec = pl.BlockSpec(memory_space=pl.ANY)
    vmem = pl.BlockSpec(memory_space=pltpu.VMEM)
    return pl.pallas_call(
        functools.partial(last_kernel, n_col),
        out_shape=[
            jax.ShapeDtypeStruct((rows, 2 * H), F32),
            jax.ShapeDtypeStruct((basis_rows, 2 * H), F32),
        ],
        in_specs=[any_spec, any_spec, vmem, vmem, vmem, pl.BlockSpec(memory_space=pltpu.SMEM)],
        out_specs=[any_spec] * 2,
        scratch_shapes=[
            pltpu.VMEM((rows, H), F32),
            pltpu.VMEM((rows, H), F32),
            pltpu.VMEM((rows, 2 * H), F32),
            pltpu.VMEM((basis_rows, 2 * H), F32),
            pltpu.VMEM((4, H, H), F32),
            pltpu.VMEM((4, H, H), F32),
            pltpu.VMEM((2 * H, 2 * H), BF16),
            pltpu.VMEM((2 * H, 2 * H), BF16),
            sem((2,)),
            sem((rows // CHUNK,)),
        ],
        compiler_params=pltpu.CompilerParams(vmem_limit_bytes=32 * 2**20),
    )(u2, l2, pack_l, pack_r, cross, orientation)


def on_device(n_col, n_row, snapshots, orientation):
    moved = first_round(n_col, n_row, snapshots, orientation)
    return tuple(last_round(n_col, n_row, *moved, orientation))


def solution(mesh):
    return jax.shard_map(
        functools.partial(on_device, mesh.shape["col"], mesh.shape["row"]),
        mesh=mesh,
        in_specs=(P("row", "col"), P()),
        out_specs=(P("row", "col"), P("row", "col")),
        check_vma=False,
    )
```

```python
import functools

import jax
import jax.numpy as jnp
from jax import lax
from jax.experimental import pallas as pl
from jax.experimental.pallas import tpu as pltpu
from jax.sharding import PartitionSpec as P

STEPS = 24
H = 128
F32 = jnp.float32
BF16 = jnp.bfloat16
MESH = pl.DeviceIdType.MESH
RAW = 1280
CHUNK = 256
OUT_CHUNK = 512
PAD = 8
UNROLL = 8
SQRT_HALF = 0.5**0.5


def angles(a, b, d):
    e = b - a
    scale = pltpu.reciprocal(jnp.maximum(jnp.abs(e), jnp.abs(d)), approx=True)
    scale = jnp.where(e >= 0.0, scale, -scale)
    e = e * scale
    dd = (d + d) * scale
    r = lax.rsqrt(e * e + dd * dd)
    cc = e * r + 1.0
    q = lax.rsqrt(cc)
    ss = dd * r
    half = q * SQRT_HALF
    return cc * half, ss * half, (ss * (q * q)) * d


def jacobi(state, a, c, d, flipped):
    lane = lax.broadcasted_iota(jnp.int32, (H, H), 1)
    row = lax.broadcasted_iota(jnp.int32, (H, H), 0)
    eye = (lane == row).astype(F32)
    zero = jnp.zeros((H, H), F32)
    ct = jnp.transpose(c)
    upper = jnp.where(flipped, d, a)
    lower = jnp.where(flipped, a, d)
    held = slice(PAD, PAD + H)
    state[0, 0, held] = upper
    state[0, 1, held] = jnp.where(flipped, ct, c)
    state[0, 2, held] = eye
    state[0, 3, held] = zero
    state[0, 4, held] = jnp.broadcast_to(jnp.sum(upper * eye, axis=1, keepdims=True), (H, H))
    state[0, 5, held] = jnp.where(flipped, c, ct)
    state[0, 6, held] = lower
    state[0, 7, held] = zero
    state[0, 8, held] = eye
    state[0, 9, held] = jnp.broadcast_to(jnp.sum(lower * eye, axis=1, keepdims=True), (H, H))

    def put(dst, k, i, f, g):
        r = PAD + 8 * i
        if i == 0:
            state[dst, k, r : r + 1] = f[:1]
            state[dst, k, r + 1 : r + 2] = g[:1]
            state[dst, k, r + 2 : r + 9] = f[1:]
            state[dst, k + 5, r : r + 7] = g[1:]
        elif i == H // 8 - 1:
            state[dst, k, r + 1 : r + 8] = f[:7]
            state[dst, k + 5, r - 1 : r + 7] = g
            state[dst, k + 5, r + 7 : r + 8] = f[7:]
        else:
            state[dst, k, r + 1 : r + 9] = f
            state[dst, k + 5, r - 1 : r + 7] = g

    def step(src, dst):
        for i in range(H // 8):
            r = slice(PAD + 8 * i, PAD + 8 * i + 8)
            u = [state[src, k, r] for k in range(5)]
            l = [state[src, k + 5, r] for k in range(5)]
            dot_ul = jnp.sum(u[2] * l[0] + u[3] * l[1], axis=1, keepdims=True)
            dot_ul = jnp.broadcast_to(dot_ul, (8, H))
            cos, sin, shift = angles(u[4], l[4], dot_ul)
            for k in range(4):
                put(dst, k, i, u[k] * cos - l[k] * sin, u[k] * sin + l[k] * cos)
            put(dst, 4, i, u[4] - shift, l[4] + shift)

    def several(_, carry):
        for _ in range(UNROLL // 2):
            step(0, 1)
            step(1, 0)
        return carry

    lax.fori_loop(0, STEPS // UNROLL, several, 0)


def final_gram(state, k):
    held = slice(PAD, PAD + H)
    y = jnp.concatenate([state[0, k, held], state[0, k + 1, held]], 1)
    w = jnp.concatenate([state[0, k + 2, held], state[0, k + 3, held]], 1)
    return lax.dot_general(
        w, y, (((1,), (1,)), ((), ())),
        precision=lax.Precision.HIGHEST, preferred_element_type=F32,
    )


def rotation(state, flipped):
    held = slice(PAD, PAD + H)
    halves = []
    for k in (2, 7):
        left, right = state[0, k, held], state[0, k + 1, held]
        halves.append(
            jnp.transpose(
                jnp.concatenate(
                    [jnp.where(flipped, right, left), jnp.where(flipped, left, right)], 1
                )
            )
        )
    return halves


def split(x):
    hi = x.astype(BF16)
    lo = (x - hi.astype(F32)).astype(BF16)
    return hi, lo


def dot(x, y):
    return lax.dot_general(x, y, (((1,), (0,)), ((), ())), preferred_element_type=F32)


def dot_t(x, y):
    return lax.dot_general(x, y, (((0,), (0,)), ((), ())), preferred_element_type=F32)


def sum_of(terms):
    while len(terms) > 1:
        terms = [sum(terms[i : i + 2][1:], terms[i]) for i in range(0, len(terms), 2)]
    return terms[0]


def product(x, w_hi, w_lo):
    hi, lo = split(x)
    return dot(hi, w_hi) + (dot(hi, w_lo) + dot(lo, w_hi))


def first_kernel(
    n_col, n_row,
    x_ref, ori_ref,
    u_out, l_out, pack_out, c_out,
    b, raw_l, raw_r, u2, l2, send_r, send_x, acc, part, rs_buf, total, state,
    pack_send, pack, w_hi, w_lo, acc2, part2, buf_0, buf_1, total2, ori,
    load_sem, rs_send, rs_recv, ag_send, ag_recv, s2_send, s2_recv, pag_send, pag_recv,
    raw_send, raw_recv, pack_ssem, pack_rsem, r_send, r_recv, x_send, out_sem,
):
    rows = b.shape[0]
    col = lax.axis_index("col")
    row = lax.axis_index("row")
    first = col == 0
    last = col == n_col - 1
    right = lax.rem(col + 1, n_col)
    left = lax.rem(col + n_col - 1, n_col)

    barrier = pltpu.get_barrier_semaphore()
    for o in range(1, n_row):
        pl.semaphore_signal(
            barrier, inc=1, device_id={"row": lax.rem(row + o, n_row)}, device_id_type=MESH
        )
    for side in (left, right):
        pl.semaphore_signal(barrier, inc=1, device_id={"col": side}, device_id_type=MESH)

    n_load = load_sem.shape[0]
    step = rows // n_load

    def load(i):
        part_rows = pl.ds(pl.multiple_of(i * step, 8), step)
        return pltpu.make_async_copy(x_ref.at[part_rows], b.at[part_rows], load_sem.at[i])

    for i in range(n_load):
        load(i).start()
    get_ori = pltpu.make_async_copy(ori_ref, ori, out_sem.at[0, rows // CHUNK])
    get_ori.start()

    def right_start(src, dst, ssem, rsem):
        @pl.when(jnp.logical_not(last))
        def _():
            pltpu.make_async_remote_copy(
                src, dst[0], ssem, rsem.at[0], device_id={"col": right}, device_id_type=MESH
            ).start()

        @pl.when(last)
        def _():
            pltpu.make_async_copy(src, dst[1], rsem.at[1]).start()

    def left_start(src, dst, ssem, rsem):
        @pl.when(jnp.logical_not(first))
        def _():
            pltpu.make_async_remote_copy(
                src, dst[1], ssem, rsem.at[1], device_id={"col": left}, device_id_type=MESH
            ).start()

        @pl.when(first)
        def _():
            pltpu.make_async_copy(src, dst[0], rsem.at[0]).start()

    def arrived(dst, sem):
        pltpu.make_async_copy(dst, dst, sem).wait()

    def right_sent(src, ssem):
        @pl.when(jnp.logical_not(last))
        def _():
            pltpu.make_async_copy(src, src, ssem).wait()

    def left_sent(src, ssem):
        @pl.when(jnp.logical_not(first))
        def _():
            pltpu.make_async_copy(src, src, ssem).wait()

    acc[...] = jnp.zeros_like(acc)

    def gram_part(i):
        load(i).wait()
        hi, lo = split(b[pl.ds(pl.multiple_of(i * step, 8), step), :])
        acc[...] += dot_t(hi, jnp.concatenate([hi, lo], 1))

    n_first = -(-RAW // step)
    lax.fori_loop(0, n_first, lambda i, c: (gram_part(i), c)[1], 0)
    pl.semaphore_wait(barrier, n_row + 1)
    raw_src = b.at[pl.ds(0, RAW)]
    right_start(raw_src, (raw_l, raw_r), raw_send.at[0], raw_recv)
    left_start(raw_src, (raw_l, raw_r), raw_send.at[1], raw_recv)
    lax.fori_loop(n_first, n_load, lambda i, c: (gram_part(i), c)[1], 0)
    cross = acc[:H, 3 * H :] + jnp.transpose(acc[H:, 2 * H : 3 * H])
    part[:H] = acc[:H, :H] + (acc[:H, 2 * H : 3 * H] + jnp.transpose(acc[:H, 2 * H : 3 * H]))
    part[H : 2 * H] = acc[:H, H : 2 * H] + cross
    part[2 * H :] = acc[H:, H : 2 * H] + (acc[H:, 3 * H :] + jnp.transpose(acc[H:, 3 * H :]))

    def all_reduce(local, buf, whole, s_send, s_recv, g_send, g_recv):
        size = buf.shape[1]
        mine = pl.ds(pl.multiple_of(row * size, 8), size)

        def scatter(o):
            peer = lax.rem(row + o, n_row)
            return pltpu.make_async_remote_copy(
                local.at[pl.ds(pl.multiple_of(peer * size, 8), size)], buf.at[o],
                s_send.at[o], s_recv.at[o], device_id={"row": peer}, device_id_type=MESH,
            )

        def gather(o):
            peer = lax.rem(row + o, n_row)
            return pltpu.make_async_remote_copy(
                whole.at[mine], whole.at[mine],
                g_send.at[o], g_recv.at[o], device_id={"row": peer}, device_id_type=MESH,
            )

        for o in range(1, n_row):
            scatter(o).start()
        value = local[mine, :]
        for o in range(1, n_row):
            scatter(o).wait_recv()
            value = value + buf[o]
        whole[mine, :] = value
        for o in range(1, n_row):
            gather(o).start()
        for o in range(1, n_row):
            gather(o).wait_recv()
        for o in range(1, n_row):
            scatter(o).wait_send()
            gather(o).wait_send()

    all_reduce(part, rs_buf, total, rs_send, rs_recv, ag_send, ag_recv)

    get_ori.wait()
    flipped = ori[0, col] == 1
    jacobi(state, total[:H], total[H : 2 * H], total[2 * H :], flipped)
    up, lo = rotation(state, flipped)
    gram_up, gram_lo = final_gram(state, 0), final_gram(state, 5)
    w_r = jnp.where(first, lo, up)
    w_x = jnp.where(first, up, lo)
    pack_send[0, : 2 * H] = w_r
    pack_send[0, 2 * H :] = jnp.where(first, gram_lo, gram_up)
    pack_send[1, : 2 * H] = w_x
    pack_send[1, 2 * H :] = jnp.where(first, gram_up, gram_lo)
    slice_rows = 3 * H // n_row
    mine = pl.ds(pl.multiple_of(row * slice_rows, 8), slice_rows)
    pack_dst = (pack.at[0, mine], pack.at[1, mine])
    right_start(pack_send.at[0, mine], pack_dst, pack_ssem.at[0], pack_rsem)
    left_start(pack_send.at[1, mine], pack_dst, pack_ssem.at[1], pack_rsem)
    hi, lo = split(jnp.concatenate([w_r, w_x], 1))
    w_hi[...] = hi
    w_lo[...] = lo

    n_turn = (rows - RAW) // CHUNK

    def late(i):
        return pl.ds(pl.multiple_of(RAW + i * CHUNK, 8), CHUNK)

    def sent(i):
        return pl.ds(pl.multiple_of(i * CHUNK, 8), CHUNK)

    def turn_part(i, carry):
        turned = product(b[late(i), :], w_hi[...], w_lo[...])
        send_r[sent(i), :] = turned[:, :H]
        send_x[sent(i), :] = turned[:, H:]
        dst = (u2.at[late(i)], l2.at[late(i)])
        right_start(send_r.at[sent(i)], dst, r_send.at[i], r_recv.at[i])
        left_start(send_x.at[sent(i)], dst, x_send.at[i], r_recv.at[i])
        return carry

    lax.fori_loop(0, n_turn, turn_part, 0)

    acc2[...] = jnp.zeros_like(acc2)

    def cross_part(at):
        u_hi, u_lo = split(u2[at, :])
        l_hi, l_lo = split(l2[at, :])
        acc2[...] += dot_t(
            jnp.concatenate([u_hi, u_lo], 1), jnp.concatenate([l_hi, l_lo], 1)
        )
        slot = at.start // CHUNK
        pltpu.make_async_copy(u2.at[at], u_out.at[at], out_sem.at[0, slot]).start()
        pltpu.make_async_copy(l2.at[at], l_out.at[at], out_sem.at[1, slot]).start()

    def pass_on(o):
        return pltpu.make_async_remote_copy(
            pack.at[:, mine], pack.at[:, mine], pag_send.at[o], pag_recv.at[o],
            device_id={"row": lax.rem(row + o, n_row)}, device_id_type=MESH,
        )

    arrived(pack_dst[0], pack_rsem.at[0])
    arrived(pack_dst[1], pack_rsem.at[1])
    for o in range(1, n_row):
        pass_on(o).start()
    arrived(raw_l, raw_recv.at[0])
    arrived(raw_r, raw_recv.at[1])
    for o in range(1, n_row):
        pass_on(o).wait_recv()
    out_pack = pltpu.make_async_copy(pack, pack_out, out_sem.at[1, rows // CHUNK])
    out_pack.start()
    wl_hi, wl_lo = split(pack[0, : 2 * H])
    wr_hi, wr_lo = split(pack[1, : 2 * H])
    w_hi[...] = jnp.concatenate([wl_hi, wr_hi], 1)
    w_lo[...] = jnp.concatenate([wl_lo, wr_lo], 1)

    def raw_part(i, carry):
        at = pl.ds(pl.multiple_of(i * CHUNK, 8), CHUNK)
        u2[at, :] = product(raw_l[at, :], w_hi[:, :H], w_lo[:, :H])
        l2[at, :] = product(raw_r[at, :], w_hi[:, H:], w_lo[:, H:])
        cross_part(at)
        return carry

    lax.fori_loop(0, RAW // CHUNK, raw_part, 0)

    def late_part(i, carry):
        arrived(u2.at[late(i)], r_recv.at[i, 0])
        arrived(l2.at[late(i)], r_recv.at[i, 1])
        cross_part(late(i))
        return carry

    lax.fori_loop(0, n_turn, late_part, 0)
    part2[...] = (acc2[:H, :H] + acc2[H:, H:]) + (acc2[:H, H:] + acc2[H:, :H])
    side = buf_0.shape[1]
    place = (lax.rem(row, side), row // side)

    def exchange(phase, half, k, src):
        axis = (phase + half) % 2
        there = lax.rem(place[axis] + k, side)
        peer = place[1] * side + there if axis == 0 else there * side + place[0]
        buf = buf_1 if phase else buf_0
        return pltpu.make_async_remote_copy(
            src, buf.at[half, place[axis]],
            s2_send.at[phase, half, k], s2_recv.at[phase, half, k],
            device_id={"row": peer}, device_id_type=MESH,
        )

    def half_of(half):
        return pl.ds(half * (H // 2), H // 2)

    order = [side // 2] + [k for k in range(1, side) if k != side // 2]
    sent_0 = [[exchange(0, h, k, part2.at[half_of(h)]) for k in order] for h in range(2)]
    for pair in zip(*sent_0):
        for copy in pair:
            copy.start()
    sent_1 = []
    for h in range(2):
        buf_0[h, place[h]] = part2[half_of(h), :]
        for copy in sent_0[h]:
            copy.wait_recv()
        buf_1[h, place[1 - h]] = sum_of([buf_0[h, k] for k in range(side)])
        sent_1.append([exchange(1, h, k, buf_1.at[h, place[1 - h]]) for k in order])
        for copy in sent_1[h]:
            copy.start()
    for h in range(2):
        for copy in sent_1[h]:
            copy.wait_recv()
        total2[half_of(h), :] = sum_of([buf_1[h, k] for k in range(side)])
    out_c = pltpu.make_async_copy(total2, c_out, load_sem.at[0])
    out_c.start()

    right_sent(raw_src, raw_send.at[0])
    left_sent(raw_src, raw_send.at[1])
    right_sent(pack_send.at[0, mine], pack_ssem.at[0])
    left_sent(pack_send.at[1, mine], pack_ssem.at[1])
    for o in range(1, n_row):
        pass_on(o).wait_send()
    for h in range(2):
        for copy in sent_0[h] + sent_1[h]:
            copy.wait_send()

    def drain(i, carry):
        right_sent(send_r.at[sent(i)], r_send.at[i])
        left_sent(send_x.at[sent(i)], x_send.at[i])
        return carry

    lax.fori_loop(0, n_turn, drain, 0)

    def written(i, carry):
        at = pl.ds(pl.multiple_of(i * CHUNK, 8), CHUNK)
        pltpu.make_async_copy(u2.at[at], u_out.at[at], out_sem.at[0, i]).wait()
        pltpu.make_async_copy(l2.at[at], l_out.at[at], out_sem.at[1, i]).wait()
        return carry

    lax.fori_loop(0, rows // CHUNK, written, 0)
    out_pack.wait()
    out_c.wait()


def first_round(n_col, n_row, snapshots, orientation):
    rows = snapshots.shape[0]
    late = rows - RAW
    n_turn = late // CHUNK
    side = 4 if n_row == 16 else 2
    sem = pltpu.SemaphoreType.DMA
    any_spec = pl.BlockSpec(memory_space=pl.ANY)
    return pl.pallas_call(
        functools.partial(first_kernel, n_col, n_row),
        out_shape=[
            jax.ShapeDtypeStruct((rows, H), F32),
            jax.ShapeDtypeStruct((rows, H), F32),
            jax.ShapeDtypeStruct((2, 3 * H, H), F32),
            jax.ShapeDtypeStruct((H, H), F32),
        ],
        in_specs=[any_spec] * 2,
        out_specs=[any_spec] * 4,
        scratch_shapes=[
            pltpu.VMEM((rows, 2 * H), F32),
            pltpu.VMEM((RAW, 2 * H), F32),
            pltpu.VMEM((RAW, 2 * H), F32),
            pltpu.VMEM((rows, H), F32),
            pltpu.VMEM((rows, H), F32),
            pltpu.VMEM((late, H), F32),
            pltpu.VMEM((late, H), F32),
            pltpu.VMEM((2 * H, 4 * H), F32),
            pltpu.VMEM((3 * H, H), F32),
            pltpu.VMEM((n_row, 3 * H // n_row, H), F32),
            pltpu.VMEM((3 * H, H), F32),
            pltpu.VMEM((2, 10, H + 2 * PAD, H), F32),
            pltpu.VMEM((2, 3 * H, H), F32),
            pltpu.VMEM((2, 3 * H, H), F32),
            pltpu.VMEM((2 * H, 2 * H), BF16),
            pltpu.VMEM((2 * H, 2 * H), BF16),
            pltpu.VMEM((2 * H, 2 * H), F32),
            pltpu.VMEM((H, H), F32),
            pltpu.VMEM((2, side, H // 2, H), F32),
            pltpu.VMEM((2, side, H // 2, H), F32),
            pltpu.VMEM((H, H), F32),
            pltpu.SMEM(orientation.shape, jnp.int32),
            sem((8,)),
            sem((n_row,)), sem((n_row,)), sem((n_row,)), sem((n_row,)),
            sem((2, 2, side)), sem((2, 2, side)), sem((n_row,)), sem((n_row,)),
            sem((2,)), sem((2,)), sem((2,)), sem((2,)),
            sem((n_turn,)), sem((n_turn, 2)), sem((n_turn,)),
            sem((2, rows // CHUNK + 1)),
        ],
        compiler_params=pltpu.CompilerParams(
            collective_id=0, has_side_effects=True, vmem_limit_bytes=48 * 2**20
        ),
    )(snapshots, orientation)


def last_kernel(
    n_col,
    u_ref, l_ref, pack_ref, c_ref, ori_ref,
    out_ref, basis_ref,
    u, l, pack, c, ori, out, basis, state, w_hi, w_lo, load_sem, out_sem,
):
    rows = u.shape[0]
    col = lax.axis_index("col")
    row = lax.axis_index("row")
    refs = (c_ref, ori_ref, pack_ref, u_ref, l_ref)
    loads = [
        pltpu.make_async_copy(src, dst, load_sem.at[i])
        for i, (src, dst) in enumerate(zip(refs, (c, ori, pack, u, l)))
    ]
    for copy in loads:
        copy.start()
    for copy in loads[:3]:
        copy.wait()
    flipped = ori[1, col] == 1
    jacobi(state, pack[0, 2 * H :], c[...], pack[1, 2 * H :], flipped)
    up, lo = rotation(state, flipped)
    hi, lo = split(jnp.concatenate([up, lo], 1))
    w_hi[...] = hi
    w_lo[...] = lo
    for copy in loads[3:]:
        copy.wait()

    def finish(i):
        at = pl.ds(i * OUT_CHUNK, OUT_CHUNK)
        return pltpu.make_async_copy(out.at[at], out_ref.at[at], out_sem.at[i])

    for i in range(rows // OUT_CHUNK):
        at = pl.ds(i * OUT_CHUNK, OUT_CHUNK)
        joined = jnp.concatenate([u[at, :], l[at, :]], 1)
        out[at, :] = product(joined, w_hi[...], w_lo[...])
        finish(i).start()

    group = row // 2
    lower_half = row % 2 == 1
    sides = []
    for side, source in ((0, jnp.maximum(col - 1, 0)), (1, jnp.minimum(col + 1, n_col - 1))):
        part = jnp.where(lower_half, pack[side, H : 2 * H], pack[side, :H])
        sides.append(jnp.where(group == source, part, 0.0))
    basis[...] = product(jnp.concatenate(sides, 1), w_hi[...], w_lo[...])
    out_basis = pltpu.make_async_copy(basis, basis_ref, load_sem.at[0])
    out_basis.start()
    for i in range(rows // OUT_CHUNK):
        finish(i).wait()
    out_basis.wait()


def last_round(n_col, n_row, u2, l2, pack, cross, orientation):
    rows = u2.shape[0]
    basis_rows = 2 * H * n_col // n_row
    sem = pltpu.SemaphoreType.DMA
    any_spec = pl.BlockSpec(memory_space=pl.ANY)
    return pl.pallas_call(
        functools.partial(last_kernel, n_col),
        out_shape=[
            jax.ShapeDtypeStruct((rows, 2 * H), F32),
            jax.ShapeDtypeStruct((basis_rows, 2 * H), F32),
        ],
        in_specs=[any_spec] * 5,
        out_specs=[any_spec] * 2,
        scratch_shapes=[
            pltpu.VMEM((rows, H), F32),
            pltpu.VMEM((rows, H), F32),
            pltpu.VMEM((2, 3 * H, H), F32),
            pltpu.VMEM((H, H), F32),
            pltpu.SMEM(orientation.shape, jnp.int32),
            pltpu.VMEM((rows, 2 * H), F32),
            pltpu.VMEM((basis_rows, 2 * H), F32),
            pltpu.VMEM((2, 10, H + 2 * PAD, H), F32),
            pltpu.VMEM((2 * H, 2 * H), BF16),
            pltpu.VMEM((2 * H, 2 * H), BF16),
            sem((5,)),
            sem((rows // OUT_CHUNK,)),
        ],
        compiler_params=pltpu.CompilerParams(vmem_limit_bytes=32 * 2**20),
    )(u2, l2, pack, cross, orientation)


def on_device(n_col, n_row, snapshots, orientation):
    moved = first_round(n_col, n_row, snapshots, orientation)
    return tuple(last_round(n_col, n_row, *moved, orientation))


def solution(mesh):
    return jax.shard_map(
        functools.partial(on_device, mesh.shape["col"], mesh.shape["row"]),
        mesh=mesh,
        in_specs=(P("row", "col"), P()),
        out_specs=(P("row", "col"), P("row", "col")),
        check_vma=False,
    )
```

```python
import functools

import jax
import jax.numpy as jnp
from jax import lax
from jax.experimental import pallas as pl
from jax.experimental.pallas import tpu as pltpu
from jax.sharding import PartitionSpec as P

STEPS = 24
H = 128
F32 = jnp.float32
BF16 = jnp.bfloat16
MESH = pl.DeviceIdType.MESH
RAW = 1536
CHUNK = 256
OUT_CHUNK = 512
RAW_CHUNK = 256
HEAD = 1
EARLY = 4
PAD = 8
UNROLL = 8
LAST_UNROLL = 24
SQRT_HALF = 0.5**0.5


def angles(a, b, d):
    e = b - a
    scale = pltpu.reciprocal(jnp.maximum(jnp.abs(e), jnp.abs(d)), approx=True)
    scale = jnp.where(e >= 0.0, scale, -scale)
    e = e * scale
    dd = (d + d) * scale
    r = lax.rsqrt(e * e + dd * dd)
    cc = e * r + 1.0
    q = lax.rsqrt(cc)
    ss = dd * r
    half = q * SQRT_HALF
    return cc * half, ss * half, (ss * (q * q)) * d


def jacobi(state, a, c, d, flipped, unroll):
    lane = lax.broadcasted_iota(jnp.int32, (H, H), 1)
    row = lax.broadcasted_iota(jnp.int32, (H, H), 0)
    eye = (lane == row).astype(F32)
    zero = jnp.zeros((H, H), F32)
    ct = jnp.transpose(c)
    upper = jnp.where(flipped, d, a)
    lower = jnp.where(flipped, a, d)
    held = slice(PAD, PAD + H)
    state[0, 0, held] = upper
    state[0, 1, held] = jnp.where(flipped, ct, c)
    state[0, 2, held] = eye
    state[0, 3, held] = zero
    state[0, 4, held] = jnp.broadcast_to(jnp.sum(upper * eye, axis=1, keepdims=True), (H, H))
    state[0, 5, held] = jnp.where(flipped, c, ct)
    state[0, 6, held] = lower
    state[0, 7, held] = zero
    state[0, 8, held] = eye
    state[0, 9, held] = jnp.broadcast_to(jnp.sum(lower * eye, axis=1, keepdims=True), (H, H))

    def put(dst, k, i, f, g):
        r = PAD + 8 * i
        if i == 0:
            state[dst, k, r : r + 1] = f[:1]
            state[dst, k, r + 1 : r + 2] = g[:1]
            state[dst, k, r + 2 : r + 9] = f[1:]
            state[dst, k + 5, r : r + 7] = g[1:]
        elif i == H // 8 - 1:
            state[dst, k, r + 1 : r + 8] = f[:7]
            state[dst, k + 5, r - 1 : r + 7] = g
            state[dst, k + 5, r + 7 : r + 8] = f[7:]
        else:
            state[dst, k, r + 1 : r + 9] = f
            state[dst, k + 5, r - 1 : r + 7] = g

    def step(src, dst):
        for i in range(H // 8):
            r = slice(PAD + 8 * i, PAD + 8 * i + 8)
            u = [state[src, k, r] for k in range(5)]
            l = [state[src, k + 5, r] for k in range(5)]
            dot_ul = jnp.sum(u[2] * l[0] + u[3] * l[1], axis=1, keepdims=True)
            dot_ul = jnp.broadcast_to(dot_ul, (8, H))
            cos, sin, shift = angles(u[4], l[4], dot_ul)
            for k in range(4):
                put(dst, k, i, u[k] * cos - l[k] * sin, u[k] * sin + l[k] * cos)
            put(dst, 4, i, u[4] - shift, l[4] + shift)

    def several(_, carry):
        for _ in range(unroll // 2):
            step(0, 1)
            step(1, 0)
        return carry

    lax.fori_loop(0, STEPS // unroll, several, 0)


def final_gram(state, k):
    held = slice(PAD, PAD + H)
    y = jnp.concatenate([state[0, k, held], state[0, k + 1, held]], 1)
    w = jnp.concatenate([state[0, k + 2, held], state[0, k + 3, held]], 1)
    return lax.dot_general(
        w, y, (((1,), (1,)), ((), ())),
        precision=lax.Precision.HIGHEST, preferred_element_type=F32,
    )


def rotation(state, flipped):
    held = slice(PAD, PAD + H)
    halves = []
    for k in (2, 7):
        left, right = state[0, k, held], state[0, k + 1, held]
        halves.append(
            jnp.transpose(
                jnp.concatenate(
                    [jnp.where(flipped, right, left), jnp.where(flipped, left, right)], 1
                )
            )
        )
    return halves


def split(x):
    hi = x.astype(BF16)
    lo = (x - hi.astype(F32)).astype(BF16)
    return hi, lo


def dot(x, y):
    return lax.dot_general(x, y, (((1,), (0,)), ((), ())), preferred_element_type=F32)


def dot_t(x, y):
    return lax.dot_general(x, y, (((0,), (0,)), ((), ())), preferred_element_type=F32)


def sum_of(terms):
    while len(terms) > 1:
        terms = [sum(terms[i : i + 2][1:], terms[i]) for i in range(0, len(terms), 2)]
    return terms[0]


def thin_product(x, w_both, w_hi):
    hi, lo = split(x)
    both = dot(hi, w_both)
    return both[:, :H] + (both[:, H:] + dot(lo, w_hi))


def product(x, w_hi, w_lo):
    hi, lo = split(x)
    return dot(hi, w_hi) + (dot(hi, w_lo) + dot(lo, w_hi))


def first_kernel(
    n_col, n_row,
    x_ref, ori_ref,
    u2, l2, pack, total2,
    b, raw_l, raw_r, send_r, send_x, acc, part, rs_buf, total, state,
    pack_send, w_hi, w_lo, v_hi, v_lo, acc2, part2, buf_0, buf_1, ori,
    load_sem, rs_send, rs_recv, ag_send, ag_recv, s2_send, s2_recv, pag_send, pag_recv,
    raw_send, raw_recv, pack_ssem, pack_rsem, r_send, r_recv, x_send, ori_sem,
):
    rows = b.shape[0]
    col = lax.axis_index("col")
    row = lax.axis_index("row")
    first = col == 0
    last = col == n_col - 1
    right = lax.rem(col + 1, n_col)
    left = lax.rem(col + n_col - 1, n_col)

    barrier = pltpu.get_barrier_semaphore()
    for side in (left, right):
        pl.semaphore_signal(barrier, inc=1, device_id={"col": side}, device_id_type=MESH)
    for o in range(1, n_row):
        pl.semaphore_signal(
            barrier, inc=1, device_id={"row": lax.rem(row + o, n_row)}, device_id_type=MESH
        )

    n_load = load_sem.shape[0]
    step = rows // n_load

    def load(i):
        part_rows = pl.ds(pl.multiple_of(i * step, 8), step)
        return pltpu.make_async_copy(x_ref.at[part_rows], b.at[part_rows], load_sem.at[i])

    for i in range(n_load):
        load(i).start()
    get_ori = pltpu.make_async_copy(ori_ref, ori, ori_sem.at[0])
    get_ori.start()

    def right_start(src, dst, ssem, rsem):
        @pl.when(jnp.logical_not(last))
        def _():
            pltpu.make_async_remote_copy(
                src, dst[0], ssem, rsem.at[0], device_id={"col": right}, device_id_type=MESH
            ).start()

        @pl.when(last)
        def _():
            pltpu.make_async_copy(src, dst[1], rsem.at[1]).start()

    def left_start(src, dst, ssem, rsem):
        @pl.when(jnp.logical_not(first))
        def _():
            pltpu.make_async_remote_copy(
                src, dst[1], ssem, rsem.at[1], device_id={"col": left}, device_id_type=MESH
            ).start()

        @pl.when(first)
        def _():
            pltpu.make_async_copy(src, dst[0], rsem.at[0]).start()

    def arrived(dst, sem):
        pltpu.make_async_copy(dst, dst, sem).wait()

    def right_sent(src, ssem):
        @pl.when(jnp.logical_not(last))
        def _():
            pltpu.make_async_copy(src, src, ssem).wait()

    def left_sent(src, ssem):
        @pl.when(jnp.logical_not(first))
        def _():
            pltpu.make_async_copy(src, src, ssem).wait()

    acc[...] = jnp.zeros_like(acc)

    def gram_part(i):
        load(i).wait()
        hi, lo = split(b[pl.ds(pl.multiple_of(i * step, 8), step), :])
        acc[...] += dot_t(hi, jnp.concatenate([hi, lo], 1))

    n_first = -(-RAW // step)
    lax.fori_loop(0, n_first, lambda i, c: (gram_part(i), c)[1], 0)
    pl.semaphore_wait(barrier, n_row + 1)
    raw_src = b.at[pl.ds(0, RAW)]
    right_start(raw_src, (raw_l, raw_r), raw_send.at[0], raw_recv)
    left_start(raw_src, (raw_l, raw_r), raw_send.at[1], raw_recv)
    lax.fori_loop(n_first, n_load, lambda i, c: (gram_part(i), c)[1], 0)
    cross = acc[:H, 3 * H :] + jnp.transpose(acc[H:, 2 * H : 3 * H])
    part[:H] = acc[:H, :H] + (acc[:H, 2 * H : 3 * H] + jnp.transpose(acc[:H, 2 * H : 3 * H]))
    part[H : 2 * H] = acc[:H, H : 2 * H] + cross
    part[2 * H :] = acc[H:, H : 2 * H] + (acc[H:, 3 * H :] + jnp.transpose(acc[H:, 3 * H :]))

    def all_reduce(local, buf, whole, s_send, s_recv, g_send, g_recv):
        size = buf.shape[1]
        mine = pl.ds(pl.multiple_of(row * size, 8), size)

        def scatter(o):
            peer = lax.rem(row + o, n_row)
            return pltpu.make_async_remote_copy(
                local.at[pl.ds(pl.multiple_of(peer * size, 8), size)], buf.at[o],
                s_send.at[o], s_recv.at[o], device_id={"row": peer}, device_id_type=MESH,
            )

        def gather(o):
            peer = lax.rem(row + o, n_row)
            return pltpu.make_async_remote_copy(
                whole.at[mine], whole.at[mine],
                g_send.at[o], g_recv.at[o], device_id={"row": peer}, device_id_type=MESH,
            )

        for o in range(1, n_row):
            scatter(o).start()
        value = local[mine, :]
        for o in range(1, n_row):
            scatter(o).wait_recv()
            value = value + buf[o]
        whole[mine, :] = value
        for o in range(1, n_row):
            gather(o).start()
        for o in range(1, n_row):
            gather(o).wait_recv()
        for o in range(1, n_row):
            scatter(o).wait_send()
            gather(o).wait_send()

    all_reduce(part, rs_buf, total, rs_send, rs_recv, ag_send, ag_recv)

    get_ori.wait()
    flipped = ori[0, col] == 1
    jacobi(state, total[:H], total[H : 2 * H], total[2 * H :], flipped, UNROLL)
    up, lo = rotation(state, flipped)
    w_r = jnp.where(first, lo, up)
    w_x = jnp.where(first, up, lo)
    hi, low = split(jnp.concatenate([w_r, w_x], 1))
    w_hi[...] = hi
    w_lo[...] = low

    n_turn = (rows - RAW) // CHUNK

    def late(i):
        return pl.ds(pl.multiple_of(RAW + i * CHUNK, 8), CHUNK)

    def sent(i):
        return pl.ds(pl.multiple_of(i * CHUNK, 8), CHUNK)

    def turn_part(i, carry):
        turned = product(b[late(i), :], w_hi[...], w_lo[...])
        send_r[sent(i), :] = turned[:, :H]
        send_x[sent(i), :] = turned[:, H:]
        dst = (u2.at[late(i)], l2.at[late(i)])
        right_start(send_r.at[sent(i)], dst, r_send.at[i], r_recv.at[i])
        left_start(send_x.at[sent(i)], dst, x_send.at[i], r_recv.at[i])
        return carry

    lax.fori_loop(0, HEAD, turn_part, 0)

    gram_up, gram_lo = final_gram(state, 0), final_gram(state, 5)
    pack_send[0, : 2 * H] = w_r
    pack_send[0, 2 * H :] = jnp.where(first, gram_lo, gram_up)
    pack_send[1, : 2 * H] = w_x
    pack_send[1, 2 * H :] = jnp.where(first, gram_up, gram_lo)
    slice_rows = 3 * H // n_row
    mine = pl.ds(pl.multiple_of(row * slice_rows, 8), slice_rows)
    pack_dst = (pack.at[0, mine], pack.at[1, mine])
    right_start(pack_send.at[0, mine], pack_dst, pack_ssem.at[0], pack_rsem)
    left_start(pack_send.at[1, mine], pack_dst, pack_ssem.at[1], pack_rsem)

    lax.fori_loop(HEAD, n_turn, turn_part, 0)

    acc2[...] = jnp.zeros_like(acc2)

    def cross_part(u, l):
        u_hi, u_lo = split(u)
        l_hi, l_lo = split(l)
        acc2[...] += dot_t(
            jnp.concatenate([u_hi, u_lo], 1), jnp.concatenate([l_hi, l_lo], 1)
        )

    def late_part(i, carry):
        arrived(u2.at[late(i)], r_recv.at[i, 0])
        arrived(l2.at[late(i)], r_recv.at[i, 1])
        cross_part(u2[late(i), :], l2[late(i), :])
        return carry

    def pass_on(o):
        return pltpu.make_async_remote_copy(
            pack.at[:, mine], pack.at[:, mine], pag_send.at[o], pag_recv.at[o],
            device_id={"row": lax.rem(row + o, n_row)}, device_id_type=MESH,
        )

    arrived(pack_dst[0], pack_rsem.at[0])
    arrived(pack_dst[1], pack_rsem.at[1])
    for o in range(1, n_row):
        pass_on(o).start()
    arrived(raw_l, raw_recv.at[0])
    arrived(raw_r, raw_recv.at[1])
    lax.fori_loop(0, EARLY, late_part, 0)
    for o in range(1, n_row):
        pass_on(o).wait_recv()
    for side, (whole, part_hi) in enumerate(((w_hi, v_hi), (w_lo, v_lo))):
        hi, low = split(pack[side, : 2 * H])
        whole[...] = jnp.concatenate([hi, low], 1)
        part_hi[...] = hi

    def raw_part(i, carry):
        at = pl.ds(pl.multiple_of(i * RAW_CHUNK, 8), RAW_CHUNK)
        u = thin_product(raw_l[at, :], w_hi[...], v_hi[...])
        l = thin_product(raw_r[at, :], w_lo[...], v_lo[...])
        u2[at, :] = u
        l2[at, :] = l
        cross_part(u, l)
        return carry

    lax.fori_loop(0, RAW // RAW_CHUNK, raw_part, 0)
    lax.fori_loop(EARLY, n_turn, late_part, 0)
    part2[...] = (acc2[:H, :H] + acc2[H:, H:]) + (acc2[:H, H:] + acc2[H:, :H])
    side = buf_0.shape[1]
    place = (lax.rem(row, side), row // side)

    def exchange(phase, half, k, src):
        axis = (phase + half) % 2
        there = lax.rem(place[axis] + k, side)
        peer = place[1] * side + there if axis == 0 else there * side + place[0]
        buf = buf_1 if phase else buf_0
        return pltpu.make_async_remote_copy(
            src, buf.at[half, place[axis]],
            s2_send.at[phase, half, k], s2_recv.at[phase, half, k],
            device_id={"row": peer}, device_id_type=MESH,
        )

    def half_of(half):
        return pl.ds(half * (H // 2), H // 2)

    order = [side // 2] + [k for k in range(1, side) if k != side // 2]
    sent_0 = [[exchange(0, h, k, part2.at[half_of(h)]) for k in order] for h in range(2)]
    for pair in zip(*sent_0):
        for copy in pair:
            copy.start()
    sent_1 = []
    for h in range(2):
        buf_0[h, place[h]] = part2[half_of(h), :]
        for copy in sent_0[h]:
            copy.wait_recv()
        buf_1[h, place[1 - h]] = sum_of([buf_0[h, k] for k in range(side)])
        sent_1.append([exchange(1, h, k, buf_1.at[h, place[1 - h]]) for k in order])
        for copy in sent_1[h]:
            copy.start()
    for h in range(2):
        for copy in sent_1[h]:
            copy.wait_recv()
        total2[half_of(h), :] = sum_of([buf_1[h, k] for k in range(side)])
    right_sent(raw_src, raw_send.at[0])
    left_sent(raw_src, raw_send.at[1])
    right_sent(pack_send.at[0, mine], pack_ssem.at[0])
    left_sent(pack_send.at[1, mine], pack_ssem.at[1])
    for o in range(1, n_row):
        pass_on(o).wait_send()
    for h in range(2):
        for copy in sent_0[h] + sent_1[h]:
            copy.wait_send()

    def drain(i, carry):
        right_sent(send_r.at[sent(i)], r_send.at[i])
        left_sent(send_x.at[sent(i)], x_send.at[i])
        return carry

    lax.fori_loop(0, n_turn, drain, 0)


def first_round(n_col, n_row, snapshots, orientation):
    rows = snapshots.shape[0]
    late = rows - RAW
    n_turn = late // CHUNK
    side = 4 if n_row == 16 else 2
    sem = pltpu.SemaphoreType.DMA
    return pl.pallas_call(
        functools.partial(first_kernel, n_col, n_row),
        out_shape=[
            jax.ShapeDtypeStruct((rows, H), F32),
            jax.ShapeDtypeStruct((rows, H), F32),
            jax.ShapeDtypeStruct((2, 3 * H, H), F32),
            jax.ShapeDtypeStruct((H, H), F32),
        ],
        in_specs=[pl.BlockSpec(memory_space=pltpu.HBM)] * 2,
        out_specs=[pl.BlockSpec(memory_space=pltpu.VMEM)] * 4,
        scratch_shapes=[
            pltpu.VMEM((rows, 2 * H), F32),
            pltpu.VMEM((RAW, 2 * H), F32),
            pltpu.VMEM((RAW, 2 * H), F32),
            pltpu.VMEM((late, H), F32),
            pltpu.VMEM((late, H), F32),
            pltpu.VMEM((2 * H, 4 * H), F32),
            pltpu.VMEM((3 * H, H), F32),
            pltpu.VMEM((n_row, 3 * H // n_row, H), F32),
            pltpu.VMEM((3 * H, H), F32),
            pltpu.VMEM((2, 10, H + 2 * PAD, H), F32),
            pltpu.VMEM((2, 3 * H, H), F32),
            pltpu.VMEM((2 * H, 2 * H), BF16),
            pltpu.VMEM((2 * H, 2 * H), BF16),
            pltpu.VMEM((2 * H, H), BF16),
            pltpu.VMEM((2 * H, H), BF16),
            pltpu.VMEM((2 * H, 2 * H), F32),
            pltpu.VMEM((H, H), F32),
            pltpu.VMEM((2, side, H // 2, H), F32),
            pltpu.VMEM((2, side, H // 2, H), F32),
            pltpu.SMEM(orientation.shape, jnp.int32),
            sem((4,)),
            sem((n_row,)), sem((n_row,)), sem((n_row,)), sem((n_row,)),
            sem((2, 2, side)), sem((2, 2, side)), sem((n_row,)), sem((n_row,)),
            sem((2,)), sem((2,)), sem((2,)), sem((2,)),
            sem((n_turn,)), sem((n_turn, 2)), sem((n_turn,)),
            sem((1,)),
        ],
        compiler_params=pltpu.CompilerParams(
            collective_id=0, has_side_effects=True, vmem_limit_bytes=48 * 2**20
        ),
    )(snapshots, orientation)


def last_kernel(
    n_col,
    u, l, pack, c, ori_ref,
    out_ref, basis_ref,
    ori, out, basis, state, w_hi, w_lo, ori_sem, out_sem,
):
    rows = u.shape[0]
    col = lax.axis_index("col")
    row = lax.axis_index("row")
    get_ori = pltpu.make_async_copy(ori_ref, ori, ori_sem.at[0])
    get_ori.start()
    get_ori.wait()
    flipped = ori[1, col] == 1
    jacobi(state, pack[0, 2 * H :], c[...], pack[1, 2 * H :], flipped, LAST_UNROLL)
    up, lo = rotation(state, flipped)
    hi, lo = split(jnp.concatenate([up, lo], 1))
    w_hi[...] = hi
    w_lo[...] = lo

    def finish(i):
        at = pl.ds(i * OUT_CHUNK, OUT_CHUNK)
        return pltpu.make_async_copy(out.at[at], out_ref.at[at], out_sem.at[i])

    for i in range(rows // OUT_CHUNK):
        at = pl.ds(i * OUT_CHUNK, OUT_CHUNK)
        joined = jnp.concatenate([u[at, :], l[at, :]], 1)
        out[at, :] = product(joined, w_hi[...], w_lo[...])
        finish(i).start()

    group = row // 2
    lower_half = row % 2 == 1
    sides = []
    for side, source in ((0, jnp.maximum(col - 1, 0)), (1, jnp.minimum(col + 1, n_col - 1))):
        part = jnp.where(lower_half, pack[side, H : 2 * H], pack[side, :H])
        sides.append(jnp.where(group == source, part, 0.0))
    basis[...] = product(jnp.concatenate(sides, 1), w_hi[...], w_lo[...])
    out_basis = pltpu.make_async_copy(basis, basis_ref, ori_sem.at[0])
    out_basis.start()
    for i in range(rows // OUT_CHUNK):
        finish(i).wait()
    out_basis.wait()


def last_round(n_col, n_row, u2, l2, pack, cross, orientation):
    rows = u2.shape[0]
    basis_rows = 2 * H * n_col // n_row
    sem = pltpu.SemaphoreType.DMA
    hbm = pl.BlockSpec(memory_space=pltpu.HBM)
    return pl.pallas_call(
        functools.partial(last_kernel, n_col),
        out_shape=[
            jax.ShapeDtypeStruct((rows, 2 * H), F32),
            jax.ShapeDtypeStruct((basis_rows, 2 * H), F32),
        ],
        in_specs=[pl.BlockSpec(memory_space=pltpu.VMEM)] * 4 + [hbm],
        out_specs=[hbm] * 2,
        scratch_shapes=[
            pltpu.SMEM(orientation.shape, jnp.int32),
            pltpu.VMEM((rows, 2 * H), F32),
            pltpu.VMEM((basis_rows, 2 * H), F32),
            pltpu.VMEM((2, 10, H + 2 * PAD, H), F32),
            pltpu.VMEM((2 * H, 2 * H), BF16),
            pltpu.VMEM((2 * H, 2 * H), BF16),
            sem((1,)),
            sem((rows // OUT_CHUNK,)),
        ],
        compiler_params=pltpu.CompilerParams(vmem_limit_bytes=48 * 2**20),
    )(u2, l2, pack, cross, orientation)


def on_device(n_col, n_row, snapshots, orientation):
    snapshots = pltpu.with_memory_space_constraint(snapshots, pltpu.HBM)
    orientation = pltpu.with_memory_space_constraint(orientation, pltpu.HBM)
    moved = first_round(n_col, n_row, snapshots, orientation)
    return tuple(last_round(n_col, n_row, *moved, orientation))


def solution(mesh):
    return jax.shard_map(
        functools.partial(on_device, mesh.shape["col"], mesh.shape["row"]),
        mesh=mesh,
        in_specs=(P("row", "col"), P()),
        out_specs=(P("row", "col"), P("row", "col")),
        check_vma=False,
    )
```

```python
import functools

import jax
import jax.numpy as jnp
from jax import lax
from jax.experimental import pallas as pl
from jax.experimental.pallas import tpu as pltpu
from jax.sharding import PartitionSpec as P

STEPS = 24
H = 128
F32 = jnp.float32
BF16 = jnp.bfloat16
MESH = pl.DeviceIdType.MESH
RAW = 1408
CHUNK = 384
OUT_CHUNK = 512
RAW_CHUNK = 352
HEAD = 1
EARLY = 3
PAD = 8
UNROLL = 8
LAST_UNROLL = 24
SQRT_HALF = 0.5**0.5
TOP = 2.0**61
FLOOR = 2.0**-62


def angles(a, b, d, scale):
    e = b - a
    size = jnp.abs(e) + FLOOR
    ds = d * jnp.where(e >= 0.0, scale, -scale)
    r = lax.rsqrt(size * size + ds * ds)
    cc = size * r + 1.0
    half = lax.rsqrt(cc) * SQRT_HALF
    s = (ds * r) * half
    return cc * half, s, (s * half) * (d * scale)


def jacobi(state, a, c, d, flipped, unroll):
    lane = lax.broadcasted_iota(jnp.int32, (H, H), 1)
    row = lax.broadcasted_iota(jnp.int32, (H, H), 0)
    eye = (lane == row).astype(F32)
    zero = jnp.zeros((H, H), F32)
    ct = jnp.transpose(c)
    upper = jnp.where(flipped, d, a)
    lower = jnp.where(flipped, a, d)
    half_a = 0.5 * jnp.sum(upper * eye, axis=1, keepdims=True)
    half_b = 0.5 * jnp.sum(lower * eye, axis=1, keepdims=True)
    total = jnp.sum(half_a + half_b, axis=0, keepdims=True)
    scale = TOP / jnp.maximum(total, 1.0 / TOP)
    held = slice(PAD, PAD + H)
    state[0, 0, held] = upper
    state[0, 1, held] = jnp.where(flipped, ct, c)
    state[0, 2, held] = eye
    state[0, 3, held] = zero
    state[0, 4, held] = jnp.broadcast_to(half_a * scale, (H, H))
    state[0, 5, held] = jnp.where(flipped, c, ct)
    state[0, 6, held] = lower
    state[0, 7, held] = zero
    state[0, 8, held] = eye
    state[0, 9, held] = jnp.broadcast_to(half_b * scale, (H, H))
    scale = jnp.broadcast_to(scale, (8, H))

    def put(dst, k, i, f, g):
        r = PAD + 8 * i
        if i == 0:
            state[dst, k, r : r + 1] = f[:1]
            state[dst, k, r + 1 : r + 2] = g[:1]
            state[dst, k, r + 2 : r + 9] = f[1:]
            state[dst, k + 5, r : r + 7] = g[1:]
        elif i == H // 8 - 1:
            state[dst, k, r + 1 : r + 8] = f[:7]
            state[dst, k + 5, r - 1 : r + 7] = g
            state[dst, k + 5, r + 7 : r + 8] = f[7:]
        else:
            state[dst, k, r + 1 : r + 9] = f
            state[dst, k + 5, r - 1 : r + 7] = g

    def step(src, dst):
        for i in range(H // 8):
            r = slice(PAD + 8 * i, PAD + 8 * i + 8)
            u = [state[src, k, r] for k in range(5)]
            l = [state[src, k + 5, r] for k in range(5)]
            dot_ul = jnp.sum(u[2] * l[0] + u[3] * l[1], axis=1, keepdims=True)
            dot_ul = jnp.broadcast_to(dot_ul, (8, H))
            cos, sin, shift = angles(u[4], l[4], dot_ul, scale)
            for k in range(4):
                put(dst, k, i, u[k] * cos - l[k] * sin, u[k] * sin + l[k] * cos)
            put(dst, 4, i, u[4] - shift, l[4] + shift)

    def several(_, carry):
        for _ in range(unroll // 2):
            step(0, 1)
            step(1, 0)
        return carry

    lax.fori_loop(0, STEPS // unroll, several, 0)


def final_gram(state, k):
    held = slice(PAD, PAD + H)
    y = jnp.concatenate([state[0, k, held], state[0, k + 1, held]], 1)
    w = jnp.concatenate([state[0, k + 2, held], state[0, k + 3, held]], 1)
    return lax.dot_general(
        w, y, (((1,), (1,)), ((), ())),
        precision=lax.Precision.HIGHEST, preferred_element_type=F32,
    )


def rotation(state, flipped):
    held = slice(PAD, PAD + H)
    halves = []
    for k in (2, 7):
        left, right = state[0, k, held], state[0, k + 1, held]
        halves.append(
            jnp.transpose(
                jnp.concatenate(
                    [jnp.where(flipped, right, left), jnp.where(flipped, left, right)], 1
                )
            )
        )
    return halves


def split(x):
    hi = x.astype(BF16)
    lo = (x - hi.astype(F32)).astype(BF16)
    return hi, lo


def dot(x, y):
    return lax.dot_general(x, y, (((1,), (0,)), ((), ())), preferred_element_type=F32)


def dot_t(x, y):
    return lax.dot_general(x, y, (((0,), (0,)), ((), ())), preferred_element_type=F32)


def sum_of(terms):
    while len(terms) > 1:
        terms = [sum(terms[i : i + 2][1:], terms[i]) for i in range(0, len(terms), 2)]
    return terms[0]


def thin_product(x, w_both, w_hi):
    hi, lo = split(x)
    both = dot(hi, w_both)
    return both[:, :H] + (both[:, H:] + dot(lo, w_hi))


def product(x, w_hi, w_lo):
    hi, lo = split(x)
    return dot(hi, w_hi) + (dot(hi, w_lo) + dot(lo, w_hi))


def first_kernel(
    n_col, n_row,
    x_ref, ori_ref,
    u2, l2, pack, total2,
    b, raw_l, raw_r, send_r, send_x, acc, part, rs_buf, total, state,
    pack_send, w_hi, w_lo, v_hi, v_lo, acc2, part2, buf_0, buf_1, ori,
    load_sem, rs_send, rs_recv, ag_send, ag_recv, s2_send, s2_recv, pag_send, pag_recv,
    raw_send, raw_recv, pack_ssem, pack_rsem, r_send, r_recv, x_send, ori_sem,
):
    rows = b.shape[0]
    col = lax.axis_index("col")
    row = lax.axis_index("row")
    first = col == 0
    last = col == n_col - 1
    right = lax.rem(col + 1, n_col)
    left = lax.rem(col + n_col - 1, n_col)

    barrier = pltpu.get_barrier_semaphore()
    for side in (left, right):
        pl.semaphore_signal(barrier, inc=1, device_id={"col": side}, device_id_type=MESH)
    for o in range(1, n_row):
        pl.semaphore_signal(
            barrier, inc=1, device_id={"row": lax.rem(row + o, n_row)}, device_id_type=MESH
        )

    n_load = load_sem.shape[0]
    step = rows // n_load

    def load(i):
        part_rows = pl.ds(pl.multiple_of(i * step, 8), step)
        return pltpu.make_async_copy(x_ref.at[part_rows], b.at[part_rows], load_sem.at[i])

    for i in range(n_load):
        load(i).start()
    get_ori = pltpu.make_async_copy(ori_ref, ori, ori_sem.at[0])
    get_ori.start()

    def right_start(src, dst, ssem, rsem):
        @pl.when(jnp.logical_not(last))
        def _():
            pltpu.make_async_remote_copy(
                src, dst[0], ssem, rsem.at[0], device_id={"col": right}, device_id_type=MESH
            ).start()

        @pl.when(last)
        def _():
            pltpu.make_async_copy(src, dst[1], rsem.at[1]).start()

    def left_start(src, dst, ssem, rsem):
        @pl.when(jnp.logical_not(first))
        def _():
            pltpu.make_async_remote_copy(
                src, dst[1], ssem, rsem.at[1], device_id={"col": left}, device_id_type=MESH
            ).start()

        @pl.when(first)
        def _():
            pltpu.make_async_copy(src, dst[0], rsem.at[0]).start()

    def arrived(dst, sem):
        pltpu.make_async_copy(dst, dst, sem).wait()

    def right_sent(src, ssem):
        @pl.when(jnp.logical_not(last))
        def _():
            pltpu.make_async_copy(src, src, ssem).wait()

    def left_sent(src, ssem):
        @pl.when(jnp.logical_not(first))
        def _():
            pltpu.make_async_copy(src, src, ssem).wait()

    acc[...] = jnp.zeros_like(acc)

    def gram_part(i):
        load(i).wait()
        hi, lo = split(b[pl.ds(pl.multiple_of(i * step, 8), step), :])
        acc[...] += dot_t(hi, jnp.concatenate([hi, lo], 1))

    n_first = -(-RAW // step)
    lax.fori_loop(0, n_first, lambda i, c: (gram_part(i), c)[1], 0)
    pl.semaphore_wait(barrier, n_row + 1)
    raw_src = b.at[pl.ds(0, RAW)]
    right_start(raw_src, (raw_l, raw_r), raw_send.at[0], raw_recv)
    left_start(raw_src, (raw_l, raw_r), raw_send.at[1], raw_recv)
    lax.fori_loop(n_first, n_load, lambda i, c: (gram_part(i), c)[1], 0)
    cross = acc[:H, 3 * H :] + jnp.transpose(acc[H:, 2 * H : 3 * H])
    part[:H] = acc[:H, :H] + (acc[:H, 2 * H : 3 * H] + jnp.transpose(acc[:H, 2 * H : 3 * H]))
    part[H : 2 * H] = acc[:H, H : 2 * H] + cross
    part[2 * H :] = acc[H:, H : 2 * H] + (acc[H:, 3 * H :] + jnp.transpose(acc[H:, 3 * H :]))

    def all_reduce(local, buf, whole, s_send, s_recv, g_send, g_recv):
        size = buf.shape[1]
        mine = pl.ds(pl.multiple_of(row * size, 8), size)

        def scatter(o):
            peer = lax.rem(row + o, n_row)
            return pltpu.make_async_remote_copy(
                local.at[pl.ds(pl.multiple_of(peer * size, 8), size)], buf.at[o],
                s_send.at[o], s_recv.at[o], device_id={"row": peer}, device_id_type=MESH,
            )

        def gather(o):
            peer = lax.rem(row + o, n_row)
            return pltpu.make_async_remote_copy(
                whole.at[mine], whole.at[mine],
                g_send.at[o], g_recv.at[o], device_id={"row": peer}, device_id_type=MESH,
            )

        for o in range(1, n_row):
            scatter(o).start()
        value = local[mine, :]
        for o in range(1, n_row):
            scatter(o).wait_recv()
            value = value + buf[o]
        whole[mine, :] = value
        for o in range(1, n_row):
            gather(o).start()
        for o in range(1, n_row):
            gather(o).wait_recv()
        return [make(o) for make in (scatter, gather) for o in range(1, n_row)]

    sums_sent = all_reduce(part, rs_buf, total, rs_send, rs_recv, ag_send, ag_recv)

    get_ori.wait()
    flipped = ori[0, col] == 1
    jacobi(state, total[:H], total[H : 2 * H], total[2 * H :], flipped, UNROLL)
    up, lo = rotation(state, flipped)
    w_r = jnp.where(first, lo, up)
    w_x = jnp.where(first, up, lo)
    hi, low = split(jnp.concatenate([w_r, w_x], 1))
    w_hi[...] = hi
    w_lo[...] = low

    n_turn = (rows - RAW) // CHUNK

    def late(i):
        return pl.ds(pl.multiple_of(RAW + i * CHUNK, 8), CHUNK)

    def sent(i):
        return pl.ds(pl.multiple_of(i * CHUNK, 8), CHUNK)

    def turn_part(i, carry):
        turned = product(b[late(i), :], w_hi[...], w_lo[...])
        send_r[sent(i), :] = turned[:, :H]
        send_x[sent(i), :] = turned[:, H:]
        dst = (u2.at[late(i)], l2.at[late(i)])
        right_start(send_r.at[sent(i)], dst, r_send.at[i], r_recv.at[i])
        left_start(send_x.at[sent(i)], dst, x_send.at[i], r_recv.at[i])
        return carry

    lax.fori_loop(0, HEAD, turn_part, 0)

    gram_up, gram_lo = final_gram(state, 0), final_gram(state, 5)
    pack_send[0, : 2 * H] = w_r
    pack_send[0, 2 * H :] = jnp.where(first, gram_lo, gram_up)
    pack_send[1, : 2 * H] = w_x
    pack_send[1, 2 * H :] = jnp.where(first, gram_up, gram_lo)
    slice_rows = 3 * H // n_row
    mine = pl.ds(pl.multiple_of(row * slice_rows, 8), slice_rows)
    pack_dst = (pack.at[0, mine], pack.at[1, mine])
    right_start(pack_send.at[0, mine], pack_dst, pack_ssem.at[0], pack_rsem)
    left_start(pack_send.at[1, mine], pack_dst, pack_ssem.at[1], pack_rsem)

    lax.fori_loop(HEAD, n_turn, turn_part, 0)

    acc2[...] = jnp.zeros_like(acc2)

    def cross_part(u, l):
        u_hi, u_lo = split(u)
        l_hi, l_lo = split(l)
        acc2[...] += dot_t(
            jnp.concatenate([u_hi, u_lo], 1), jnp.concatenate([l_hi, l_lo], 1)
        )

    def late_part(i, carry):
        arrived(u2.at[late(i)], r_recv.at[i, 0])
        arrived(l2.at[late(i)], r_recv.at[i, 1])
        cross_part(u2[late(i), :], l2[late(i), :])
        return carry

    def pass_on(o):
        return pltpu.make_async_remote_copy(
            pack.at[:, mine], pack.at[:, mine], pag_send.at[o], pag_recv.at[o],
            device_id={"row": lax.rem(row + o, n_row)}, device_id_type=MESH,
        )

    arrived(pack_dst[0], pack_rsem.at[0])
    arrived(pack_dst[1], pack_rsem.at[1])
    for o in range(1, n_row):
        pass_on(o).start()
    arrived(raw_l, raw_recv.at[0])
    arrived(raw_r, raw_recv.at[1])
    lax.fori_loop(0, EARLY, late_part, 0)
    for o in range(1, n_row):
        pass_on(o).wait_recv()
    for side, (whole, part_hi) in enumerate(((w_hi, v_hi), (w_lo, v_lo))):
        hi, low = split(pack[side, : 2 * H])
        whole[...] = jnp.concatenate([hi, low], 1)
        part_hi[...] = hi

    def raw_part(i, carry):
        at = pl.ds(pl.multiple_of(i * RAW_CHUNK, 8), RAW_CHUNK)
        u = thin_product(raw_l[at, :], w_hi[...], v_hi[...])
        l = thin_product(raw_r[at, :], w_lo[...], v_lo[...])
        u2[at, :] = u
        l2[at, :] = l
        cross_part(u, l)
        return carry

    lax.fori_loop(0, RAW // RAW_CHUNK, raw_part, 0)
    lax.fori_loop(EARLY, n_turn, late_part, 0)
    part2[...] = (acc2[:H, :H] + acc2[H:, H:]) + (acc2[:H, H:] + acc2[H:, :H])
    side = buf_0.shape[1]
    place = (lax.rem(row, side), row // side)

    def exchange(phase, half, k, src):
        axis = (phase + half) % 2
        there = lax.rem(place[axis] + k, side)
        peer = place[1] * side + there if axis == 0 else there * side + place[0]
        buf = buf_1 if phase else buf_0
        return pltpu.make_async_remote_copy(
            src, buf.at[half, place[axis]],
            s2_send.at[phase, half, k], s2_recv.at[phase, half, k],
            device_id={"row": peer}, device_id_type=MESH,
        )

    def half_of(half):
        return pl.ds(half * (H // 2), H // 2)

    order = [side // 2] + [k for k in range(1, side) if k != side // 2]
    sent_0 = [[exchange(0, h, k, part2.at[half_of(h)]) for k in order] for h in range(2)]
    for pair in zip(*sent_0):
        for copy in pair:
            copy.start()
    for copy in sums_sent:
        copy.wait_send()
    right_sent(raw_src, raw_send.at[0])
    left_sent(raw_src, raw_send.at[1])
    right_sent(pack_send.at[0, mine], pack_ssem.at[0])
    left_sent(pack_send.at[1, mine], pack_ssem.at[1])
    for o in range(1, n_row):
        pass_on(o).wait_send()
    def drain(i, carry):
        right_sent(send_r.at[sent(i)], r_send.at[i])
        left_sent(send_x.at[sent(i)], x_send.at[i])
        return carry

    lax.fori_loop(0, n_turn, drain, 0)

    sent_1 = []
    for h in range(2):
        buf_0[h, place[h]] = part2[half_of(h), :]
        for copy in sent_0[h]:
            copy.wait_recv()
        buf_1[h, place[1 - h]] = sum_of([buf_0[h, k] for k in range(side)])
        sent_1.append([exchange(1, h, k, buf_1.at[h, place[1 - h]]) for k in order])
        for copy in sent_1[h]:
            copy.start()
    for h in range(2):
        for copy in sent_1[h]:
            copy.wait_recv()
        total2[half_of(h), :] = sum_of([buf_1[h, k] for k in range(side)])
    for h in range(2):
        for copy in sent_0[h] + sent_1[h]:
            copy.wait_send()


def first_round(n_col, n_row, snapshots, orientation):
    rows = snapshots.shape[0]
    late = rows - RAW
    n_turn = late // CHUNK
    side = 4 if n_row == 16 else 2
    sem = pltpu.SemaphoreType.DMA
    return pl.pallas_call(
        functools.partial(first_kernel, n_col, n_row),
        out_shape=[
            jax.ShapeDtypeStruct((rows, H), F32),
            jax.ShapeDtypeStruct((rows, H), F32),
            jax.ShapeDtypeStruct((2, 3 * H, H), F32),
            jax.ShapeDtypeStruct((H, H), F32),
        ],
        in_specs=[pl.BlockSpec(memory_space=pltpu.HBM)] * 2,
        out_specs=[pl.BlockSpec(memory_space=pltpu.VMEM)] * 4,
        scratch_shapes=[
            pltpu.VMEM((rows, 2 * H), F32),
            pltpu.VMEM((RAW, 2 * H), F32),
            pltpu.VMEM((RAW, 2 * H), F32),
            pltpu.VMEM((late, H), F32),
            pltpu.VMEM((late, H), F32),
            pltpu.VMEM((2 * H, 4 * H), F32),
            pltpu.VMEM((3 * H, H), F32),
            pltpu.VMEM((n_row, 3 * H // n_row, H), F32),
            pltpu.VMEM((3 * H, H), F32),
            pltpu.VMEM((2, 10, H + 2 * PAD, H), F32),
            pltpu.VMEM((2, 3 * H, H), F32),
            pltpu.VMEM((2 * H, 2 * H), BF16),
            pltpu.VMEM((2 * H, 2 * H), BF16),
            pltpu.VMEM((2 * H, H), BF16),
            pltpu.VMEM((2 * H, H), BF16),
            pltpu.VMEM((2 * H, 2 * H), F32),
            pltpu.VMEM((H, H), F32),
            pltpu.VMEM((2, side, H // 2, H), F32),
            pltpu.VMEM((2, side, H // 2, H), F32),
            pltpu.SMEM(orientation.shape, jnp.int32),
            sem((4,)),
            sem((n_row,)), sem((n_row,)), sem((n_row,)), sem((n_row,)),
            sem((2, 2, side)), sem((2, 2, side)), sem((n_row,)), sem((n_row,)),
            sem((2,)), sem((2,)), sem((2,)), sem((2,)),
            sem((n_turn,)), sem((n_turn, 2)), sem((n_turn,)),
            sem((1,)),
        ],
        compiler_params=pltpu.CompilerParams(
            collective_id=0, has_side_effects=True, vmem_limit_bytes=48 * 2**20
        ),
    )(snapshots, orientation)


def last_kernel(
    n_col,
    u, l, pack, c, ori_ref,
    out_ref, basis_ref,
    ori, out, basis, state, w_hi, w_lo, ori_sem, out_sem,
):
    rows = u.shape[0]
    col = lax.axis_index("col")
    row = lax.axis_index("row")
    get_ori = pltpu.make_async_copy(ori_ref, ori, ori_sem.at[0])
    get_ori.start()
    get_ori.wait()
    flipped = ori[1, col] == 1
    jacobi(state, pack[0, 2 * H :], c[...], pack[1, 2 * H :], flipped, LAST_UNROLL)
    up, lo = rotation(state, flipped)
    hi, lo = split(jnp.concatenate([up, lo], 1))
    w_hi[...] = hi
    w_lo[...] = lo

    def finish(i):
        at = pl.ds(i * OUT_CHUNK, OUT_CHUNK)
        return pltpu.make_async_copy(out.at[at], out_ref.at[at], out_sem.at[i])

    for i in range(rows // OUT_CHUNK):
        at = pl.ds(i * OUT_CHUNK, OUT_CHUNK)
        joined = jnp.concatenate([u[at, :], l[at, :]], 1)
        out[at, :] = product(joined, w_hi[...], w_lo[...])
        finish(i).start()

    group = row // 2
    lower_half = row % 2 == 1
    sides = []
    for side, source in ((0, jnp.maximum(col - 1, 0)), (1, jnp.minimum(col + 1, n_col - 1))):
        part = jnp.where(lower_half, pack[side, H : 2 * H], pack[side, :H])
        sides.append(jnp.where(group == source, part, 0.0))
    basis[...] = product(jnp.concatenate(sides, 1), w_hi[...], w_lo[...])
    out_basis = pltpu.make_async_copy(basis, basis_ref, ori_sem.at[0])
    out_basis.start()
    for i in range(rows // OUT_CHUNK):
        finish(i).wait()
    out_basis.wait()


def last_round(n_col, n_row, u2, l2, pack, cross, orientation):
    rows = u2.shape[0]
    basis_rows = 2 * H * n_col // n_row
    sem = pltpu.SemaphoreType.DMA
    hbm = pl.BlockSpec(memory_space=pltpu.HBM)
    return pl.pallas_call(
        functools.partial(last_kernel, n_col),
        out_shape=[
            jax.ShapeDtypeStruct((rows, 2 * H), F32),
            jax.ShapeDtypeStruct((basis_rows, 2 * H), F32),
        ],
        in_specs=[pl.BlockSpec(memory_space=pltpu.VMEM)] * 4 + [hbm],
        out_specs=[hbm] * 2,
        scratch_shapes=[
            pltpu.SMEM(orientation.shape, jnp.int32),
            pltpu.VMEM((rows, 2 * H), F32),
            pltpu.VMEM((basis_rows, 2 * H), F32),
            pltpu.VMEM((2, 10, H + 2 * PAD, H), F32),
            pltpu.VMEM((2 * H, 2 * H), BF16),
            pltpu.VMEM((2 * H, 2 * H), BF16),
            sem((1,)),
            sem((rows // OUT_CHUNK,)),
        ],
        compiler_params=pltpu.CompilerParams(vmem_limit_bytes=48 * 2**20),
    )(u2, l2, pack, cross, orientation)


def on_device(n_col, n_row, snapshots, orientation):
    snapshots = pltpu.with_memory_space_constraint(snapshots, pltpu.HBM)
    orientation = pltpu.with_memory_space_constraint(orientation, pltpu.HBM)
    moved = first_round(n_col, n_row, snapshots, orientation)
    return tuple(last_round(n_col, n_row, *moved, orientation))


def solution(mesh):
    return jax.shard_map(
        functools.partial(on_device, mesh.shape["col"], mesh.shape["row"]),
        mesh=mesh,
        in_specs=(P("row", "col"), P()),
        out_specs=(P("row", "col"), P("row", "col")),
        check_vma=False,
    )
```
